32 devices in a mesh: groups: 2 (over x), req: 16 (over z, y, core).
Axes of the slice: x: 2, y: 2, z: 4, core: 2. Of those that a mesh axis runs over, the one named last changes fastest.
Arguments:
- saved_hidden: bfloat16 [2048, 8, 8192], P(('groups', 'req')), parts along dimension 0, may hold values from -6 to 6
- kv_weight: bfloat16 [8192, 1024], replicated, may hold values from -0.0625 to 0.0625
- queries: bfloat16 [128, 4096], P(('groups', 'req')), parts along dimension 0, may hold values from -30 to 30
- new_kv: bfloat16 [128, 1024], P(('groups', 'req')), parts along dimension 0, may hold values from -3 to 3
- hist_blocks: int32 [8], P('groups'), parts along dimension 0, may hold values from 1 to 256, 512 in all
- new_len: int32 [8], P('groups'), parts along dimension 0, may hold values from 1 to 16, 48 in all
- pack_order: int32 [8], P('groups'), parts along dimension 0, may hold values from 0 to 3, each once
- holder_slot: int32 [1024], P('groups'), parts along dimension 0, may hold values from 0 to 1023, as said below
Outputs:
- restored_cache: bfloat16 [1024, 8, 1024], P(('groups', 'req')), parts along dimension 0
- attention: bfloat16 [128, 4096], P(('groups', 'req')), parts along dimension 0
The draws below stay inside these ranges and needn't reach their ends.
There are 2 independent parts, one for each index of `groups`. The reference program is written for one: setup_inputs(seed, part) draws one part's arguments, and reference() takes and returns one part's arrays. A program takes and returns all parts, laid end to end along the dimension named above; an argument that names none is the same for every part. Nothing has to cross between parts.
Inputs may be any that keep to these rules, and one draw needn't show every extreme that they name: `hist_blocks`: their sum is 512. `new_len`: their sum is three quarters of 64, rounded down. `pack_order`: A permutation of the requests. Device holder_slot // 64 of req keeps block g's saved rows at its local slot holder_slot % 64; no slot holds two blocks. Exactly half of the devices of req hold saved blocks, the first and the last device among them, each 64 blocks; of the 32 blocks n * 32 to (n + 1) * 32 - 1, each such device holds exactly 4, for every n.
All inputs are finite; a program needn't handle non-finite values.
Results may differ from the reference program's by a relative error of at most 0.01.
The reference program's roundings to bfloat16 on the way (of `new_rows`, `query_rot` and `rounded`) count: a program that leaves them out, or rounds other values in their place, can miss the bound.
Values may be sent and summed in bfloat16 or wider, within the bound.
No kernel may reach another device: no remote copies, remote signals or barrier semaphores. Data moves between devices by JAX's collectives and lax.ppermute only.
A program may use at most 128 MiB of HBM per device.

```python
import math
import jax
import jax.numpy as jnp
import numpy as np
from jax import lax

D = 8192
KVH = 4
QPK = 8
HD = 128
BLK = 8
NEWT = 16
OWN = 32
REQS = 4
NB = 512
HOLD = 64
CAP = 4
SLOTS = 1024
MAXB = 256
NEWTOK = 64
N_REQ = 16


rope_base = 500000.0


def shared_signs(key):
    return (jax.random.randint(key, (REQS, KVH, HD), 0, 2) * 2 - 1).astype(jnp.float32)


def strengths():
    return 10.0 * (1.0 + (jnp.arange(REQS) % 3).astype(jnp.float32))


def turn_one(sign_table):
    half_width = HD // 2
    frequency = rope_base ** (-(jnp.arange(half_width, dtype=jnp.float32) * 2.0 / HD))
    cosine = jnp.cos(frequency)
    sine_part = jnp.sin(frequency)
    first_half = sign_table[..., :half_width]
    second_half = sign_table[..., half_width:]
    return jnp.concatenate([first_half * cosine - second_half * sine_part, second_half * cosine + first_half * sine_part], axis=-1)


def draw_new_kv(key, part):
    sign_table = shared_signs(key)
    key = jax.random.fold_in(key, 5)
    full_shape = (REQS, NEWT, 2, KVH, HD)
    values = jnp.clip(jax.random.normal(key, full_shape, jnp.float32), -3.0, 3.0)
    shrink = 1.0 - 2.0 / (strengths() * HD ** 0.5)
    values = values.at[:, 1, 0].set(sign_table)
    values = values.at[:, 0, 0].set(turn_one(sign_table) * shrink[:, None, None])
    return values.reshape(NEWTOK, 2 * KVH * HD).astype(jnp.bfloat16)


def draw_queries(key, part):
    sign_table = shared_signs(key)
    key = jax.random.fold_in(key, 7)
    full_shape = (REQS, NEWT, KVH, QPK, HD)
    values = jnp.clip(jax.random.normal(key, full_shape, jnp.float32), -3.0, 3.0)
    aligned = strengths()[:, None, None, None] * sign_table[:, :, None, :]
    values = values.at[:, 1].set(jnp.broadcast_to(aligned, (REQS, KVH, QPK, HD)))
    opposed = -(30.0 / 2.0 ** 0.5) * turn_one(sign_table)[:, :, None, :]
    opposed = jnp.clip(opposed, -30.0, 30.0)
    values = values.at[:, 0].set(jnp.broadcast_to(opposed, (REQS, KVH, QPK, HD)))
    return values.reshape(NEWTOK, KVH * QPK * HD).astype(jnp.bfloat16)


def draw_holder_slot(key, part):
    key = jax.random.fold_in(key, 11)
    first_key, second_key, third_key, fourth_key = jax.random.split(key, 4)
    half_count = N_REQ // 2
    middle = (jax.random.permutation(first_key, N_REQ - 2) + 1).astype(jnp.int32)
    holders = jnp.concatenate([jnp.array([0, N_REQ - 1], dtype=jnp.int32), middle[:half_count - 2]])
    holders = jax.random.permutation(third_key, holders)
    owner_order = jax.random.permutation(second_key, N_REQ).astype(jnp.int32)
    shifts = jax.random.randint(fourth_key, (N_REQ,), 0, OWN)
    slot_ids = jnp.arange(N_REQ * OWN, dtype=jnp.int32)
    owners = slot_ids // OWN
    within = (slot_ids % OWN + shifts[owners]) % OWN
    storage_rank = owner_order[owners] * CAP + within // half_count
    return (holders[within % half_count] * HOLD + storage_rank).astype(jnp.int32)


def levels(own_key, shape, cuts, low, top_value):
    def one(position, blocks):
        steps = jax.random.uniform(jax.random.fold_in(jax.random.fold_in(own_key, 6), position), (blocks,), jnp.float32, low / len(cuts), top_value / len(cuts))
        return jnp.repeat(jnp.exp(steps), shape[position] // blocks).reshape((-1,) + (1,) * (len(shape) - position - 1))

    loudness = one(*cuts[0])
    for cut in cuts[1:]:
        loudness = loudness * one(*cut)
    return loudness


def length_profile(amount, total, reach, skew):
    loads = [(1 << 20) // math.isqrt(grade ** skew) + 1 for grade in range(2, amount + 1)]
    rest, given = total - reach - (amount - 1), [1] * (amount - 1)
    while rest > 0:
        movable = [i for i in range(amount - 1) if given[i] < reach]
        mass, remaining = sum([loads[i] for i in movable]), rest
        for i in movable:
            more = min(reach - given[i], max(1, remaining * loads[i] // mass), rest)
            given[i] = given[i] + more
            rest = rest - more
    return np.array([reach] + given)


def ragged_sizes(own_key, count, total, most, lean):
    if count == 2:
        one = jax.random.randint(own_key, (), max(1, total - most), min(most, total - 1) + 1)
        return jnp.stack([one, total - one])
    sizes = jnp.asarray(length_profile(count, total, most, lean), jnp.int32)
    couples = (count - 1) // 2
    giver, taker = sizes[1:1 + 2 * couples:2], sizes[2:2 + 2 * couples:2]
    room = jnp.minimum(giver - 1, most - taker)
    moved = jax.random.randint(jax.random.fold_in(own_key, 1), (couples,), 0, 1 << 20) % (room + 1)
    sizes = sizes.at[1:1 + 2 * couples:2].set(giver - moved).at[2:2 + 2 * couples:2].set(taker + moved)
    return sizes[jax.random.permutation(jax.random.fold_in(own_key, 2), count)]


def scatter_about(stream_key, dims, deviation, bound, shards=(), kind=jnp.bfloat16):
    level = levels(stream_key, dims, shards, -0.22, 0.18) if shards else 1.0
    entries = jax.random.normal(stream_key, dims, jnp.float32) * deviation * level
    return jnp.minimum(jnp.maximum(entries, -bound), bound).astype(kind)


def setup_inputs(seed: int = 0, part: int = 0) -> dict:
    key_list = jax.random.split(jax.random.key(seed), 9)
    part_splits = jax.random.split(jax.random.fold_in(key_list[8], part), 9)
    return {
        "saved_hidden": scatter_about(part_splits[0], (SLOTS, BLK, D), 1.0, 6.0, ((0, 16),)),
        "kv_weight": scatter_about(key_list[1], (D, 2 * KVH * HD), D ** -0.5, 0.0625),
        "queries": draw_queries(jax.random.fold_in(jax.random.fold_in(key_list[8], part), 71), part),
        "new_kv": draw_new_kv(jax.random.fold_in(jax.random.fold_in(key_list[8], part), 71), part),
        "hist_blocks": ragged_sizes(part_splits[4], REQS, NB, MAXB, 2).astype(jnp.int32),
        "new_len": ragged_sizes(part_splits[5], REQS, REQS * NEWT * 3 // 4, NEWT, 1).astype(jnp.int32),
        "pack_order": jax.random.permutation(part_splits[6], REQS).astype(jnp.int32),
        "holder_slot": draw_holder_slot(jax.random.fold_in(jax.random.fold_in(key_list[8], part), 71), part),
    }


rope_base = 500000.0
masked_score = -1e30


def rotate(values, positions):
    half_width = HD // 2
    frequency = rope_base ** (-(jnp.arange(half_width, dtype=jnp.float32) * 2.0 / HD))
    angles = positions.astype(jnp.float32)[..., None] * frequency
    cosine = jnp.cos(angles)
    sine_part = jnp.sin(angles)
    first_half = values[..., :half_width]
    second_half = values[..., half_width:]
    return jnp.concatenate([first_half * cosine - second_half * sine_part, second_half * cosine + first_half * sine_part], axis=-1)


def layout(hist_blocks, pack_order):
    request_ids = jnp.arange(hist_blocks.shape[0], dtype=jnp.int32)
    onehot = (pack_order[:, None] == request_ids[None, :]).astype(jnp.int32)
    ordered = jnp.sum(onehot * hist_blocks[None, :], axis=1).astype(jnp.int32)
    ordered_start = (jnp.cumsum(ordered) - ordered).astype(jnp.int32)
    request_start = jnp.sum(onehot * ordered_start[:, None], axis=0).astype(jnp.int32)
    request_place = jnp.sum(onehot * request_ids[:, None], axis=0).astype(jnp.int32)
    return request_start, request_place


def slot_tables(request_start, hist_blocks, slot_ids):
    block_end = request_start + hist_blocks
    inside = ((slot_ids[:, None] >= request_start[None, :]) & (slot_ids[:, None] < block_end[None, :])).astype(jnp.int32)
    request_ids = jnp.arange(hist_blocks.shape[0], dtype=jnp.int32)
    slot_request = jnp.sum(inside * request_ids[None, :], axis=1).astype(jnp.int32)
    slot_block = (slot_ids - jnp.sum(inside * request_start[None, :], axis=1)).astype(jnp.int32)
    return slot_request, slot_block


def finish(projected, positions):
    key_width = KVH * HD
    lead_shape = projected.shape[:-1]
    rotated = rotate(projected[..., :key_width].reshape(lead_shape + (KVH, HD)), positions[..., None])
    rotated = rotated.reshape(lead_shape + (key_width,))
    return jnp.concatenate([rotated, projected[..., key_width:]], axis=-1).astype(jnp.bfloat16)


def partial_softmax(query_rot, key_rows, allowed):
    key_count = key_rows.shape[0]
    key_width = KVH * HD
    key_part = key_rows[:, :key_width].reshape(key_count, KVH, HD).astype(jnp.float32)
    value_part = key_rows[:, key_width:].reshape(key_count, KVH, HD).astype(jnp.float32)
    scores = jnp.einsum("tgjd,sgd->gjts", query_rot.astype(jnp.float32), key_part) * (HD ** -0.5)
    scores = jnp.where(allowed[None, None], scores, masked_score)
    peak = jnp.max(scores, axis=-1)
    weights = jnp.exp(scores - peak[..., None])
    denominator = jnp.sum(weights, axis=-1)
    rounded = lax.optimization_barrier(weights.astype(jnp.bfloat16)).astype(jnp.float32)
    numerator = jnp.einsum("gjts,sgd->tgjd", rounded, value_part)
    tokens = query_rot.shape[0]
    head_count = KVH * QPK
    return (jnp.transpose(peak, (2, 0, 1)).reshape(tokens, head_count),
            jnp.transpose(denominator, (2, 0, 1)).reshape(tokens, head_count),
            numerator.reshape(tokens, head_count, HD))


def reference(saved_hidden, kv_weight, queries, new_kv, hist_blocks, new_len, pack_order, holder_slot):
    block_rows = saved_hidden.shape[1]
    slot_count = holder_slot.shape[0]
    pair_width = kv_weight.shape[1]
    request_start, request_place = layout(hist_blocks, pack_order)
    slot_request, slot_block = slot_tables(request_start, hist_blocks, jnp.arange(slot_count, dtype=jnp.int32))
    row_ids = jnp.arange(block_rows, dtype=jnp.int32)

    def restore_group(group):
        sources, blocks = group
        hidden = saved_hidden[sources]
        projected = jnp.dot(hidden.reshape(-1, hidden.shape[2]), kv_weight, preferred_element_type=jnp.float32)
        projected = projected.reshape(OWN, block_rows, pair_width)
        positions = blocks[:, None] * block_rows + row_ids[None, :]
        return finish(projected, positions)

    restored = lax.map(restore_group, (holder_slot.reshape(-1, OWN), slot_block.reshape(-1, OWN)))
    restored = restored.reshape(slot_count, block_rows, pair_width)

    flat = jnp.concatenate([restored.reshape(-1, pair_width), jnp.zeros((MAXB * block_rows, pair_width), jnp.bfloat16)], axis=0)
    offsets = jnp.arange(NEWT, dtype=jnp.int32)
    history_ids = jnp.arange(MAXB * block_rows, dtype=jnp.int32)

    def attend(request):
        history = hist_blocks[request]
        live_new = new_len[request]
        new_positions = history * block_rows + offsets
        keys_hist = lax.dynamic_slice_in_dim(flat, request_start[request] * block_rows, MAXB * block_rows, 0)
        query_rows = lax.dynamic_slice_in_dim(queries, request * NEWT, NEWT, 0).astype(jnp.float32).reshape(NEWT, KVH, QPK, HD)
        query_rot = lax.optimization_barrier(rotate(query_rows, new_positions[:, None, None]).astype(jnp.bfloat16))
        new_rows = finish(lax.dynamic_slice_in_dim(new_kv, request * NEWT, NEWT, 0).astype(jnp.float32), new_positions)
        key_rows = lax.optimization_barrier(jnp.concatenate([keys_hist, new_rows], axis=0))
        hist_ok = history_ids < history * block_rows
        new_ok = (offsets[None, :] <= offsets[:, None]) & (offsets[None, :] < live_new)
        allowed = jnp.concatenate([jnp.broadcast_to(hist_ok[None, :], (NEWT, hist_ok.shape[0])), new_ok], axis=1)
        peak, denominator, numerator = partial_softmax(query_rot, key_rows, allowed)
        output = numerator / denominator[..., None]
        output = jnp.where((offsets < live_new)[:, None, None], output, 0.0)
        return output.reshape(NEWT, KVH * QPK * HD).astype(jnp.bfloat16)

    attention = lax.map(attend, jnp.arange(REQS, dtype=jnp.int32)).reshape(REQS * NEWT, KVH * QPK * HD)
    return restored, attention
```

```python
import functools

import jax
import jax.numpy as jnp
import numpy as np
from jax import lax
from jax.experimental import pallas as pl
from jax.experimental.pallas import tpu as pltpu
from jax.sharding import PartitionSpec as P

KVH = 4
QPK = 8
HD = 128
NEWT = 16
ROPE_BASE = 500000.0
MASKED = -1e30
SCALE = HD ** -0.5
F32 = jnp.float32
BF16 = jnp.bfloat16
I32 = jnp.int32
HALF = KVH * HD
LAYER = 4
ATTEND_WORK = 60 * 10**9
VM = pltpu.VMEM
SM = pltpu.SMEM
ANY = pl.ANY
HBM = pltpu.HBM


def frequencies():
    wave = ROPE_BASE ** (-(np.arange(HD // 2, dtype=np.float64) * 2.0 / HD))
    return np.concatenate([wave, wave]).astype(np.float32)[None, :]


def lane_sign(shape):
    lanes = lax.broadcasted_iota(I32, shape, len(shape) - 1)
    return jnp.where(lanes < HD // 2, -1.0, 1.0).astype(F32)


def specs(*spaces):
    return [pl.BlockSpec(memory_space=space) for space in spaces]


def call(kernel, name, inputs, spaces, outputs, out_spaces, scratch=(), mib=16, work=0):
    return pl.pallas_call(
        kernel,
        out_shape=tuple(jax.ShapeDtypeStruct(shape, kind) for shape, kind in outputs),
        in_specs=specs(*spaces),
        out_specs=tuple(specs(*out_spaces)),
        scratch_shapes=list(scratch),
        compiler_params=pltpu.CompilerParams(vmem_limit_bytes=mib << 20),
        cost_estimate=pl.CostEstimate(flops=work, transcendentals=0, bytes_accessed=0) if work else None,
        name=name,
    )(*inputs)


def split_sizes(width):
    return tuple(width // 16 * units for units in (1, 2, 3, 3, 3, 2, 2))


def iota(shape, axis):
    return lax.broadcasted_iota(I32, shape, axis)


def lane_total(values):
    return jnp.sum(values, axis=1, keepdims=True)


def spans(hist_ref, pack_ref):
    start = jnp.int32(0)
    for position in range(hist_ref.shape[0]):
        which = pack_ref[position]
        stop = start + hist_ref[which]
        yield which, start, stop
        start = stop


def places(device, holder, hist_ref, pack_ref, hold, owned, capacity):
    total = holder.shape[1]
    local = holder - device * hold
    held = (local >= 0) & (local < hold)
    blocks = iota((hold, total), 1)
    here = local == iota((hold, total), 0)
    block = lane_total(jnp.where(here, blocks, 0).astype(F32)).astype(I32)
    owner = block // owned
    rank = lane_total(jnp.where(held & (blocks < block) & (blocks >= owner * owned), 1.0, 0.0)).astype(I32)
    target = jnp.minimum(owner * capacity + jnp.minimum(rank, capacity - 1), hold - 1)
    target = jnp.where(lane_total(jnp.where(here, 1.0, 0.0)) > 0, target, iota((hold, 1), 0))
    depth = jnp.zeros((hold, 1), I32)
    for _, start, stop in spans(hist_ref, pack_ref):
        depth = jnp.where((block >= start) & (block < stop), block - start, depth)
    mine = device * owned
    blocks = iota((owned, total), 1)
    rows = iota((owned, total), 0) + mine
    keeper = holder // hold
    kept = lane_total(jnp.where(blocks == rows, keeper, 0).astype(F32)).astype(I32)
    order = lane_total(jnp.where((keeper == kept) & (blocks >= mine) & (blocks < rows), 1.0, 0.0)).astype(I32)
    arrival = kept * capacity + jnp.minimum(order, capacity - 1)
    arrival = jnp.concatenate([arrival, jnp.zeros((hold - owned, 1), I32)], axis=0)
    diagonal = iota((hold, HD), 0) == iota((hold, HD), 1)
    rows = [jnp.sum(jnp.where(diagonal, column, 0).astype(F32), axis=0, keepdims=True) for column in (target, arrival)]
    table = jnp.concatenate(rows + [jnp.zeros((6, HD), F32)], axis=0).astype(I32)
    return table, depth


def row_tags(device, holder, hist_ref, pack_ref, hold, block_rows):
    total = holder.shape[1]
    blocks = iota((8, total), 1)
    request = jnp.zeros((8, total), F32)
    for which, start, stop in spans(hist_ref, pack_ref):
        request = jnp.where((blocks >= start) & (blocks < stop), (which + 1).astype(F32), request)
    local = holder - device * hold
    match = local == iota((hold * block_rows, total), 0) // block_rows
    return lax.dot_general(
        request.astype(BF16), match.astype(F32).astype(BF16), (((1,), (1,)), ((), ())), preferred_element_type=F32
    )


def project_kernel(owned, capacity, hist_hbm, pack_hbm, len_hbm, holder_hbm, wave_hbm, new_hbm, rows_hbm, weight_hbm,
                   pairs, table_out, tags, turns,
                   rows_buf, weight_buf, total, fresh, hist_ref, pack_ref, len_ref, holder_ref, wave_ref, new_ref,
                   small_sem, rows_sem, weight_sem):
    hold, block_rows, width = rows_hbm.shape
    small = [
        pltpu.make_async_copy(source, target, small_sem.at[index])
        for index, (source, target) in enumerate((
            (hist_hbm, hist_ref), (pack_hbm, pack_ref), (len_hbm, len_ref), (holder_hbm, holder_ref),
            (wave_hbm, wave_ref), (new_hbm, new_ref),
        ))
    ]
    for copy in small:
        copy.start()
    copies, offset = [], 0
    for part, size in enumerate(split_sizes(width)):
        span = pl.ds(offset, size)
        copies.append((
            offset,
            size,
            pltpu.make_async_copy(weight_hbm.at[span, :], weight_buf.at[span, :], weight_sem.at[part]),
            pltpu.make_async_copy(rows_hbm.at[:, :, span], rows_buf.at[:, :, span], rows_sem.at[part]),
        ))
        offset += size

    def depart(part):
        if part < len(copies):
            for copy in copies[part][2:]:
                copy.start()

    depart(0)
    depart(1)

    def multiply(part, lanes):
        offset, size, _, _ = copies[part]
        left = rows_buf[:, :, offset:offset + size].reshape(hold * block_rows, size)
        product = jnp.dot(left, weight_buf[offset:offset + size, lanes], preferred_element_type=F32)
        return product if part == 0 else total[:, lanes] + product

    def arrive(part):
        for copy in copies[part][2:]:
            copy.wait()
        depart(part + 2)

    everything = slice(0, 2 * HALF)
    for part in range(2):
        arrive(part)
        total[...] = multiply(part, everything)
    for copy in small:
        copy.wait()
    device = lax.axis_index("req")
    holder = holder_ref[...]
    found, depth = places(device, holder, hist_ref, pack_ref, hold, owned, capacity)
    table_out[...] = found
    tags[0:8, :] = row_tags(device, holder, hist_ref, pack_ref, hold, block_rows)
    tags[8:16, :] = row_tags(device ^ 1, holder, hist_ref, pack_ref, hold, block_rows)
    wave = wave_ref[...]
    sign = lane_sign((block_rows, HD))
    angle = (depth * block_rows).astype(F32) * wave
    block_cos, block_sin = jnp.cos(angle)[:, None, :], jnp.sin(angle)[:, None, :]
    angle = iota((block_rows, HD), 0).astype(F32) * wave
    row_cos, row_sin = jnp.cos(angle)[None], jnp.sin(angle)[None]
    cosine = (block_cos * row_cos - block_sin * row_sin).reshape(-1, HD)
    sine = ((block_sin * row_cos + block_cos * row_sin) * sign[None]).reshape(-1, HD)
    tokens = new_ref.shape[0]
    first = device * tokens
    place = iota((block_rows, HD), 0) + (hist_ref[first // NEWT] * block_rows + first % NEWT)
    angle = place.astype(F32) * wave
    new_cos, new_sin = jnp.cos(angle), jnp.sin(angle) * sign
    for group in range(turns.shape[0]):
        request = (first // NEWT) ^ group
        place = iota((8, HD), 0) % tokens + (hist_ref[request] * block_rows + first % NEWT)
        angle = place.astype(F32) * wave
        turns[group, 0] = jnp.cos(angle)
        turns[group, 1] = jnp.sin(angle) * lane_sign((8, HD))
        tags[pl.ds(16 + group, 1), :] = jnp.full((1, tags.shape[1]), len_ref[request].astype(F32))
    fresh[...] = jnp.zeros_like(fresh)
    fresh[0:tokens, :] = new_ref[...].astype(F32)
    for head in range(KVH):
        lanes = slice(head * HD, (head + 1) * HD)
        part = fresh[:, lanes]
        pairs[hold, :, lanes] = (part * new_cos + pltpu.roll(part, HD // 2, 1) * new_sin).astype(BF16)
    pairs[hold, :, HALF:] = fresh[:, HALF:].astype(BF16)
    last = len(copies) - 1
    for part in range(2, last):
        arrive(part)
        total[...] = multiply(part, everything)
    arrive(last)
    for head in range(2 * KVH):
        lanes = slice(head * HD, (head + 1) * HD)
        if head % KVH == 0:
            half = slice(head * HD, (head + KVH) * HD)
            total[:, half] = multiply(last, half)
        part = total[:, lanes]
        if head < KVH:
            part = part * cosine + pltpu.roll(part, HD // 2, 1) * sine
        pairs[0:hold, :, lanes] = part.astype(BF16).reshape(hold, block_rows, HD)


def ship_kernel(groups, table_hbm, pairs, turns, *refs):
    queries, (outgoing, turned, rows, table, table_sem, send_sem) = refs[:groups], refs[groups:]
    table_copy = pltpu.make_async_copy(table_hbm, table, table_sem)
    table_copy.start()
    hold = outgoing.shape[0]
    tokens = queries[0].shape[0]

    def turn(group):
        values = queries[group][...].astype(F32)
        for head in range(KVH * QPK):
            rows[group, pl.ds(head * tokens, tokens), :] = values[:, head * HD:(head + 1) * HD]
        flat = rows[group]
        swapped = pltpu.roll(flat, HD // 2, 1)
        result = flat.reshape(-1, 8, HD) * turns[group, 0][None] + swapped.reshape(-1, 8, HD) * turns[group, 1][None]
        turned[:, group] = result.reshape(KVH, QPK * tokens, HD).astype(BF16)

    for group in range(groups // 2):
        turn(group)
    table_copy.wait()

    def send(slot, carry):
        pltpu.make_async_copy(pairs.at[slot], outgoing.at[table[0, slot]], send_sem).start()
        return carry

    lax.fori_loop(0, hold, send, 0)
    for group in range(groups // 2, groups):
        turn(group)
    pltpu.make_async_copy(pairs.at[pl.ds(0, hold)], outgoing, send_sem).wait()


def encode(level):
    lanes = iota(level.shape, 1)
    high = level.astype(BF16).astype(F32)
    rest = level - high
    middle = rest.astype(BF16).astype(F32)
    low = rest - middle
    packed = jnp.where(lanes < 32, high, jnp.where(lanes < 64, pltpu.roll(middle, 32, 1), pltpu.roll(low, 64, 1)))
    return jnp.where(lanes < 96, packed, 0.0).astype(BF16)


def decode(packed):
    packed = packed.astype(F32)
    return packed + (pltpu.roll(packed, HD - 32, 1) + pltpu.roll(packed, HD - 64, 1))


def folding_order(groups):
    if groups == 1:
        return [0]
    inner = folding_order(groups // 2)
    return [2 * group for group in inner] + [2 * group + 1 for group in inner]


def attend_kernel(groups, tokens, queries, queries_across, pairs, pairs_beside, tags, keep, send):
    hold, block_rows = pairs.shape[0] - 1, pairs.shape[1]
    rows_kept = hold * block_rows
    span = QPK * tokens
    rows = 2 * groups * span
    device = lax.axis_index("req")
    per_request = NEWT // tokens
    request = device // per_request
    row = iota((rows, 1), 0)
    group = (row // span) % groups
    wanted = ((request ^ group) + 1).astype(F32)
    tag_rows = [tags[0:1, :], tags[8:9, :]]
    row_all = iota((rows, 2 * block_rows), 0)
    column = iota((rows, 2 * block_rows), 1)
    across = row_all // (groups * span)
    query_place = ((device ^ (2 * across)) % per_request) * tokens + row_all % tokens
    key_index = column % block_rows
    key_place = ((device ^ (column // block_rows)) % per_request) * tokens + key_index
    fresh_ok = (
        ((row_all // span) % groups == 0) & (key_index < tokens) & (key_place <= query_place)
        & (key_place.astype(F32) < tags[16:17, 0:1])
    )
    limit = jnp.zeros((rows, 1), F32)
    for layer in range(groups):
        limit = jnp.where(group == layer, tags[16 + layer:17 + layer, 0:1], limit)
    side = row // (groups * span)
    live = (((device ^ (2 * side)) % per_request) * tokens + row % tokens).astype(F32) < limit
    lanes = iota((rows, HD), 1)
    levels = jnp.zeros((rows, HD), F32)
    for head in range(KVH):
        key_lanes = slice(head * HD, (head + 1) * HD)
        value_lanes = slice(HALF + head * HD, HALF + (head + 1) * HD)
        query = jnp.concatenate(
            [queries[head].reshape(groups * span, HD), queries_across[head].reshape(groups * span, HD)], axis=0
        )
        scores, values = [], []
        for source, tag in zip((pairs, pairs_beside), tag_rows):
            keys = source[0:hold, :, key_lanes].reshape(rows_kept, HD)
            part = lax.dot_general(query, keys, (((1,), (1,)), ((), ())), preferred_element_type=F32) * SCALE
            scores.append(jnp.where(tag == wanted, part, MASKED))
            values.append(source[0:hold, :, value_lanes].reshape(rows_kept, HD))
        keys = jnp.concatenate([pairs[hold, :, key_lanes], pairs_beside[hold, :, key_lanes]], axis=0)
        part = lax.dot_general(query, keys, (((1,), (1,)), ((), ())), preferred_element_type=F32) * SCALE
        scores.append(jnp.where(fresh_ok, part, MASKED))
        values.append(jnp.concatenate([pairs[hold, :, value_lanes], pairs_beside[hold, :, value_lanes]], axis=0))
        peak = jnp.max(jnp.maximum(scores[0], scores[1]), axis=1, keepdims=True)
        peak = jnp.maximum(peak, jnp.max(scores[2], axis=1, keepdims=True))
        weights = [jnp.exp(part - peak) for part in scores]
        denominator = lane_total(weights[0] + weights[1]) + lane_total(weights[2])
        sums = None
        for weight, value in zip(weights, values):
            part = jnp.dot(weight.astype(BF16), value, preferred_element_type=F32)
            sums = part if sums is None else sums + part
        sums = jnp.where(live, sums / denominator, 0.0).astype(BF16).reshape(2, groups, span, HD)
        for place, group in enumerate(folding_order(groups)):
            keep[place, head] = sums[0, group]
            send[place, head] = sums[1, group]
        levels = jnp.where(lanes == head, peak + jnp.log(denominator), levels)
    packed = encode(levels).reshape(2, groups, span, HD)
    for place, group in enumerate(folding_order(groups)):
        keep[place, KVH] = packed[0, group]
        send[place, KVH] = packed[1, group]


def merge(parts):
    levels = [decode(part[KVH]) for part in parts]
    top = functools.reduce(jnp.maximum, levels)
    scales = [jnp.exp(level - top) for level in levels]
    whole = functools.reduce(jnp.add, scales)
    scales = [scale / whole for scale in scales]
    heads = []
    for head in range(KVH):
        pieces = [part[head].astype(F32) * scale[:, head:head + 1] for part, scale in zip(parts, scales)]
        heads.append(functools.reduce(jnp.add, pieces))
    return heads, top + jnp.log(whole)


def fold_kernel(kept, received, keep, send):
    count = kept.shape[0]
    for group in range(count):
        heads, level = merge([kept[group], received[group]])
        out, index = (keep, group) if group < count // 2 else (send, group - count // 2)
        for head in range(KVH):
            out[index, head] = heads[head].astype(BF16)
        out[index, KVH] = encode(level)


def finish_kernel(tokens, *refs):
    parts, out = refs[:-1], refs[-1]
    heads, _ = merge([part[0] for part in parts])
    for head in range(KVH):
        for inner in range(QPK):
            start = (head * QPK + inner) * HD
            out[:, start:start + HD] = heads[head][inner * tokens:(inner + 1) * tokens, :].astype(BF16)


def settle_kernel(table, incoming, out, sem):
    def place(block, carry):
        pltpu.make_async_copy(incoming.at[table[1, block]], out.at[block], sem).start()
        return carry

    lax.fori_loop(0, out.shape[0], place, 0)
    pltpu.make_async_copy(incoming.at[pl.ds(0, out.shape[0])], out, sem).wait()


def on_device(
    saved_hidden, kv_weight, queries, new_kv, hist_blocks, new_len, pack_order, holder_slot
):
    count = lax.axis_size("req")
    hold, block_rows, width = saved_hidden.shape
    pair_width = kv_weight.shape[1]
    owned = holder_slot.shape[0] // count
    capacity = hold // count
    tokens, query_width = queries.shape
    groups = count // LAYER
    span = QPK * tokens
    wave = jnp.asarray(frequencies())

    def swap(value, flip):
        return lax.ppermute(value, "req", [(i, i ^ flip) for i in range(count)])

    layers = [queries] + [swap(queries, LAYER * group) for group in range(1, groups)]
    chunks = len(split_sizes(width))
    pairs, table, tags, turns = call(
        functools.partial(project_kernel, owned, capacity),
        "project",
        tuple(
            pltpu.with_memory_space_constraint(value, HBM)
            for value in (
                hist_blocks, pack_order, new_len, holder_slot.reshape(1, -1), wave, new_kv, saved_hidden, kv_weight
            )
        ),
        (HBM,) * 8,
        (
            ((hold + 1, block_rows, pair_width), BF16),
            ((8, HD), I32),
            ((16 + groups, hold * block_rows), F32),
            ((groups, 2, 8, HD), F32),
        ),
        (VM,) * 4,
        (
            VM((hold, block_rows, width), BF16),
            VM((width, pair_width), BF16),
            VM((hold * block_rows, pair_width), F32),
            VM((block_rows, pair_width), F32),
            SM(hist_blocks.shape, I32),
            SM(pack_order.shape, I32),
            SM(new_len.shape, I32),
            VM((1, holder_slot.shape[0]), I32),
            VM(wave.shape, F32),
            VM(new_kv.shape, BF16),
            pltpu.SemaphoreType.DMA((6,)),
            pltpu.SemaphoreType.DMA((chunks,)),
            pltpu.SemaphoreType.DMA((chunks,)),
        ),
        34,
    )
    outgoing, turned = call(
        functools.partial(ship_kernel, groups),
        "ship",
        (table, pairs, turns, *layers),
        (ANY,) + (VM,) * (groups + 2),
        (
            ((hold, block_rows, pair_width), BF16),
            ((KVH, groups, span, HD), BF16),
        ),
        (ANY, VM),
        (
            VM((groups, KVH * span, HD), F32),
            SM((8, HD), I32),
            pltpu.SemaphoreType.DMA(()),
            pltpu.SemaphoreType.DMA(()),
        ),
    )
    outgoing, pairs, turned = lax.optimization_barrier((outgoing, pairs, turned))
    pairs_beside = swap(pairs, 1)
    turned_across = swap(turned, 2)
    incoming = lax.all_to_all(outgoing, "req", split_axis=0, concat_axis=0, tiled=True)
    share = ((groups, KVH + 1, span, HD), BF16)
    keep, send = call(
        functools.partial(attend_kernel, groups, tokens),
        "attend",
        (turned, turned_across, pairs, pairs_beside, tags),
        (VM,) * 5,
        (share, share),
        (VM, VM),
        mib=24,
        work=ATTEND_WORK,
    )
    step, left = 2, groups
    while left > 1:
        left //= 2
        share = ((left, KVH + 1, span, HD), BF16)
        keep, send = call(fold_kernel, "fold", (keep, swap(send, step)), (VM, VM), (share, share), (VM, VM))
        step *= 2
    parts = [keep, swap(send, step)]
    (restored,) = call(
        settle_kernel,
        "settle",
        (table, incoming),
        (SM, ANY),
        (((owned, block_rows, pair_width), BF16),),
        (ANY,),
        (pltpu.SemaphoreType.DMA(()),),
    )
    parts, restored = lax.optimization_barrier((parts, restored))
    (attention,) = call(
        functools.partial(finish_kernel, tokens),
        "finish",
        tuple(parts),
        (VM, VM),
        (((tokens, query_width), BF16),),
        (VM,),
    )
    return restored, attention


def solution(mesh):
    return jax.shard_map(
        on_device,
        mesh=mesh,
        in_specs=(
            P(("groups", "req"), None, None),
            P(),
            P(("groups", "req"), None),
            P(("groups", "req"), None),
            P("groups"),
            P("groups"),
            P("groups"),
            P("groups"),
        ),
        out_specs=(P(("groups", "req"), None, None), P(("groups", "req"), None)),
        check_vma=False,
    )
```

```python
import functools

import jax
import jax.numpy as jnp
import numpy as np
from jax import lax
from jax.experimental import pallas as pl
from jax.experimental.pallas import tpu as pltpu
from jax.sharding import PartitionSpec as P

KVH = 4
QPK = 8
HD = 128
NEWT = 16
ROPE_BASE = 500000.0
MASKED = -1e30
SCALE = HD ** -0.5
F32 = jnp.float32
BF16 = jnp.bfloat16
I32 = jnp.int32
HALF = KVH * HD
LAYER = 4
ATTEND_WORK = 60 * 10**9
VM = pltpu.VMEM
SM = pltpu.SMEM
ANY = pl.ANY
HBM = pltpu.HBM


def frequencies():
    wave = ROPE_BASE ** (-(np.arange(HD // 2, dtype=np.float64) * 2.0 / HD))
    return np.concatenate([wave, wave]).astype(np.float32)[None, :]


def lane_sign(shape):
    lanes = lax.broadcasted_iota(I32, shape, len(shape) - 1)
    return jnp.where(lanes < HD // 2, -1.0, 1.0).astype(F32)


def specs(*spaces):
    return [pl.BlockSpec(memory_space=space) for space in spaces]


def call(kernel, name, inputs, spaces, outputs, out_spaces, scratch=(), mib=16, work=0):
    return pl.pallas_call(
        kernel,
        out_shape=tuple(jax.ShapeDtypeStruct(shape, kind) for shape, kind in outputs),
        in_specs=specs(*spaces),
        out_specs=tuple(specs(*out_spaces)),
        scratch_shapes=list(scratch),
        compiler_params=pltpu.CompilerParams(vmem_limit_bytes=mib << 20),
        cost_estimate=pl.CostEstimate(flops=work, transcendentals=0, bytes_accessed=0) if work else None,
        name=name,
    )(*inputs)


def split_sizes(width):
    return tuple(width // 16 * units for units in (1, 2, 3, 3, 3, 2, 2))


def iota(shape, axis):
    return lax.broadcasted_iota(I32, shape, axis)


def lane_total(values):
    return jnp.sum(values, axis=1, keepdims=True)


def spans(hist_ref, pack_ref):
    start = jnp.int32(0)
    for position in range(hist_ref.shape[0]):
        which = pack_ref[position]
        stop = start + hist_ref[which]
        yield which, start, stop
        start = stop


def places(device, holder, hist_ref, pack_ref, hold, owned, capacity):
    total = holder.shape[1]
    local = holder - device * hold
    held = (local >= 0) & (local < hold)
    blocks = iota((hold, total), 1)
    here = local == iota((hold, total), 0)
    block = lane_total(jnp.where(here, blocks, 0).astype(F32)).astype(I32)
    owner = block // owned
    rank = lane_total(jnp.where(held & (blocks < block) & (blocks >= owner * owned), 1.0, 0.0)).astype(I32)
    target = jnp.clip(hold - (owner + 1) * capacity + jnp.minimum(rank, capacity - 1), 0, hold - 1)
    target = jnp.where(lane_total(jnp.where(here, 1.0, 0.0)) > 0, target, iota((hold, 1), 0))
    depth = jnp.zeros((hold, 1), I32)
    for _, start, stop in spans(hist_ref, pack_ref):
        depth = jnp.where((block >= start) & (block < stop), block - start, depth)
    mine = device * owned
    blocks = iota((owned, total), 1)
    rows = iota((owned, total), 0) + mine
    keeper = holder // hold
    kept = lane_total(jnp.where(blocks == rows, keeper, 0).astype(F32)).astype(I32)
    order = lane_total(jnp.where((keeper == kept) & (blocks >= mine) & (blocks < rows), 1.0, 0.0)).astype(I32)
    arrival = hold - (kept + 1) * capacity + jnp.minimum(order, capacity - 1)
    arrival = jnp.concatenate([arrival, jnp.zeros((hold - owned, 1), I32)], axis=0)
    diagonal = iota((hold, HD), 0) == iota((hold, HD), 1)
    rows = [jnp.sum(jnp.where(diagonal, column, 0).astype(F32), axis=0, keepdims=True) for column in (target, arrival)]
    table = jnp.concatenate(rows + [jnp.zeros((6, HD), F32)], axis=0).astype(I32)
    return table, depth


def row_tags(device, holder, hist_ref, pack_ref, hold, block_rows):
    total = holder.shape[1]
    blocks = iota((8, total), 1)
    request = jnp.zeros((8, total), F32)
    for which, start, stop in spans(hist_ref, pack_ref):
        request = jnp.where((blocks >= start) & (blocks < stop), (which + 1).astype(F32), request)
    local = holder - device * hold
    match = local == iota((hold * block_rows, total), 0) // block_rows
    return lax.dot_general(
        request.astype(BF16), match.astype(F32).astype(BF16), (((1,), (1,)), ((), ())), preferred_element_type=F32
    )


def project_kernel(owned, capacity, hist_hbm, pack_hbm, len_hbm, holder_hbm, wave_hbm, new_hbm, rows_hbm, weight_hbm,
                   pairs, table_out, tags, turns,
                   rows_buf, weight_buf, total, fresh, hist_ref, pack_ref, len_ref, holder_ref, wave_ref, new_ref,
                   small_sem, rows_sem, weight_sem):
    hold, block_rows, width = rows_hbm.shape
    small = [
        pltpu.make_async_copy(source, target, small_sem.at[index])
        for index, (source, target) in enumerate((
            (hist_hbm, hist_ref), (pack_hbm, pack_ref), (len_hbm, len_ref), (holder_hbm, holder_ref),
            (wave_hbm, wave_ref), (new_hbm, new_ref),
        ))
    ]
    for copy in small:
        copy.start()
    copies, offset = [], 0
    for part, size in enumerate(split_sizes(width)):
        span = pl.ds(offset, size)
        copies.append((
            offset,
            size,
            pltpu.make_async_copy(weight_hbm.at[span, :], weight_buf.at[span, :], weight_sem.at[part]),
            pltpu.make_async_copy(rows_hbm.at[:, :, span], rows_buf.at[:, :, span], rows_sem.at[part]),
        ))
        offset += size

    def depart(part):
        if part < len(copies):
            for copy in copies[part][2:]:
                copy.start()

    depart(0)
    depart(1)

    def multiply(part, lanes):
        offset, size, _, _ = copies[part]
        left = rows_buf[:, :, offset:offset + size].reshape(hold * block_rows, size)
        product = jnp.dot(left, weight_buf[offset:offset + size, lanes], preferred_element_type=F32)
        return product if part == 0 else total[:, lanes] + product

    def arrive(part):
        for copy in copies[part][2:]:
            copy.wait()
        depart(part + 2)

    everything = slice(0, 2 * HALF)
    for part in range(2):
        arrive(part)
        total[...] = multiply(part, everything)
    for copy in small:
        copy.wait()
    device = lax.axis_index("req")
    holder = holder_ref[...]
    found, depth = places(device, holder, hist_ref, pack_ref, hold, owned, capacity)
    table_out[...] = found
    tags[0:8, :] = row_tags(device, holder, hist_ref, pack_ref, hold, block_rows)
    tags[8:16, :] = row_tags(device ^ 1, holder, hist_ref, pack_ref, hold, block_rows)
    wave = wave_ref[...]
    sign = lane_sign((block_rows, HD))
    angle = (depth * block_rows).astype(F32) * wave
    block_cos, block_sin = jnp.cos(angle)[:, None, :], jnp.sin(angle)[:, None, :]
    angle = iota((block_rows, HD), 0).astype(F32) * wave
    row_cos, row_sin = jnp.cos(angle)[None], jnp.sin(angle)[None]
    cosine = (block_cos * row_cos - block_sin * row_sin).reshape(-1, HD)
    sine = ((block_sin * row_cos + block_cos * row_sin) * sign[None]).reshape(-1, HD)
    tokens = new_ref.shape[0]
    first = device * tokens
    place = iota((block_rows, HD), 0) + (hist_ref[first // NEWT] * block_rows + first % NEWT)
    angle = place.astype(F32) * wave
    new_cos, new_sin = jnp.cos(angle), jnp.sin(angle) * sign
    for group in range(turns.shape[0]):
        request = (first // NEWT) ^ group
        place = iota((8, HD), 0) % tokens + (hist_ref[request] * block_rows + first % NEWT)
        angle = place.astype(F32) * wave
        turns[group, 0] = jnp.cos(angle)
        turns[group, 1] = jnp.sin(angle) * lane_sign((8, HD))
        tags[pl.ds(16 + group, 1), :] = jnp.full((1, tags.shape[1]), len_ref[request].astype(F32))
    fresh[...] = jnp.zeros_like(fresh)
    fresh[0:tokens, :] = new_ref[...].astype(F32)
    for head in range(KVH):
        lanes = slice(head * HD, (head + 1) * HD)
        part = fresh[:, lanes]
        pairs[hold, :, lanes] = (part * new_cos + pltpu.roll(part, HD // 2, 1) * new_sin).astype(BF16)
    pairs[hold, :, HALF:] = fresh[:, HALF:].astype(BF16)
    last = len(copies) - 1
    for part in range(2, last):
        arrive(part)
        total[...] = multiply(part, everything)
    arrive(last)
    for head in range(2 * KVH):
        lanes = slice(head * HD, (head + 1) * HD)
        if head % KVH == 0:
            half = slice(head * HD, (head + KVH) * HD)
            total[:, half] = multiply(last, half)
        part = total[:, lanes]
        if head < KVH:
            part = part * cosine + pltpu.roll(part, HD // 2, 1) * sine
        pairs[0:hold, :, lanes] = part.astype(BF16).reshape(hold, block_rows, HD)


def ship_kernel(groups, table_hbm, pairs, turns, *refs):
    queries, (outgoing, turned, rows, table, table_sem, send_sem) = refs[:groups], refs[groups:]
    table_copy = pltpu.make_async_copy(table_hbm, table, table_sem)
    table_copy.start()
    hold = outgoing.shape[0]
    tokens = queries[0].shape[0]

    def turn(group):
        values = queries[group][...].astype(F32)
        for head in range(KVH * QPK):
            rows[group, pl.ds(head * tokens, tokens), :] = values[:, head * HD:(head + 1) * HD]
        flat = rows[group]
        swapped = pltpu.roll(flat, HD // 2, 1)
        result = flat.reshape(-1, 8, HD) * turns[group, 0][None] + swapped.reshape(-1, 8, HD) * turns[group, 1][None]
        turned[:, group] = result.reshape(KVH, QPK * tokens, HD).astype(BF16)

    for group in range(groups // 2):
        turn(group)
    table_copy.wait()

    def send(slot, carry):
        pltpu.make_async_copy(pairs.at[slot], outgoing.at[table[0, slot]], send_sem).start()
        return carry

    lax.fori_loop(0, hold, send, 0)
    for group in range(groups // 2, groups):
        turn(group)
    pltpu.make_async_copy(pairs.at[pl.ds(0, hold)], outgoing, send_sem).wait()


def encode(level):
    lanes = iota(level.shape, 1)
    high = level.astype(BF16).astype(F32)
    rest = level - high
    middle = rest.astype(BF16).astype(F32)
    low = rest - middle
    packed = jnp.where(lanes < 32, high, jnp.where(lanes < 64, pltpu.roll(middle, 32, 1), pltpu.roll(low, 64, 1)))
    return jnp.where(lanes < 96, packed, 0.0).astype(BF16)


def decode(packed):
    packed = packed.astype(F32)
    return packed + (pltpu.roll(packed, HD - 32, 1) + pltpu.roll(packed, HD - 64, 1))


def folding_order(groups):
    if groups == 1:
        return [0]
    inner = folding_order(groups // 2)
    return [2 * group for group in inner] + [2 * group + 1 for group in inner]


def attend_kernel(groups, tokens, queries, queries_across, pairs, pairs_beside, tags, keep, send):
    hold, block_rows = pairs.shape[0] - 1, pairs.shape[1]
    rows_kept = hold * block_rows
    span = QPK * tokens
    rows = 2 * groups * span
    device = lax.axis_index("req")
    per_request = NEWT // tokens
    request = device // per_request
    row = iota((rows, 1), 0)
    group = (row // span) % groups
    wanted = ((request ^ group) + 1).astype(F32)
    tag_rows = [tags[0:1, :], tags[8:9, :]]
    row_all = iota((rows, 2 * block_rows), 0)
    column = iota((rows, 2 * block_rows), 1)
    across = row_all // (groups * span)
    query_place = ((device ^ (2 * across)) % per_request) * tokens + row_all % tokens
    key_index = column % block_rows
    key_place = ((device ^ (column // block_rows)) % per_request) * tokens + key_index
    fresh_ok = (
        ((row_all // span) % groups == 0) & (key_index < tokens) & (key_place <= query_place)
        & (key_place.astype(F32) < tags[16:17, 0:1])
    )
    limit = jnp.zeros((rows, 1), F32)
    for layer in range(groups):
        limit = jnp.where(group == layer, tags[16 + layer:17 + layer, 0:1], limit)
    side = row // (groups * span)
    live = (((device ^ (2 * side)) % per_request) * tokens + row % tokens).astype(F32) < limit
    lanes = iota((rows, HD), 1)
    levels = jnp.zeros((rows, HD), F32)
    for head in range(KVH):
        key_lanes = slice(head * HD, (head + 1) * HD)
        value_lanes = slice(HALF + head * HD, HALF + (head + 1) * HD)
        query = jnp.concatenate(
            [queries[head].reshape(groups * span, HD), queries_across[head].reshape(groups * span, HD)], axis=0
        )
        scores, values = [], []
        for source, tag in zip((pairs, pairs_beside), tag_rows):
            keys = source[0:hold, :, key_lanes].reshape(rows_kept, HD)
            part = lax.dot_general(query, keys, (((1,), (1,)), ((), ())), preferred_element_type=F32) * SCALE
            scores.append(jnp.where(tag == wanted, part, MASKED))
            values.append(source[0:hold, :, value_lanes].reshape(rows_kept, HD))
        keys = jnp.concatenate([pairs[hold, :, key_lanes], pairs_beside[hold, :, key_lanes]], axis=0)
        part = lax.dot_general(query, keys, (((1,), (1,)), ((), ())), preferred_element_type=F32) * SCALE
        scores.append(jnp.where(fresh_ok, part, MASKED))
        values.append(jnp.concatenate([pairs[hold, :, value_lanes], pairs_beside[hold, :, value_lanes]], axis=0))
        peak = jnp.max(jnp.maximum(scores[0], scores[1]), axis=1, keepdims=True)
        peak = jnp.maximum(peak, jnp.max(scores[2], axis=1, keepdims=True))
        weights = [jnp.exp(part - peak) for part in scores]
        denominator = lane_total(weights[0] + weights[1]) + lane_total(weights[2])
        sums = None
        for weight, value in zip(weights, values):
            part = jnp.dot(weight.astype(BF16), value, preferred_element_type=F32)
            sums = part if sums is None else sums + part
        sums = jnp.where(live, sums / denominator, 0.0).astype(BF16).reshape(2, groups, span, HD)
        for place, group in enumerate(folding_order(groups)):
            keep[place, head] = sums[0, group]
            send[place, head] = sums[1, group]
        levels = jnp.where(lanes == head, peak + jnp.log(denominator), levels)
    packed = encode(levels).reshape(2, groups, span, HD)
    for place, group in enumerate(folding_order(groups)):
        keep[place, KVH] = packed[0, group]
        send[place, KVH] = packed[1, group]


def merge(parts):
    levels = [decode(part[KVH]) for part in parts]
    top = functools.reduce(jnp.maximum, levels)
    scales = [jnp.exp(level - top) for level in levels]
    whole = functools.reduce(jnp.add, scales)
    scales = [scale / whole for scale in scales]
    heads = []
    for head in range(KVH):
        pieces = [part[head].astype(F32) * scale[:, head:head + 1] for part, scale in zip(parts, scales)]
        heads.append(functools.reduce(jnp.add, pieces))
    return heads, top + jnp.log(whole)


def fold_kernel(kept, received, keep, send):
    count = kept.shape[0]
    for group in range(count):
        heads, level = merge([kept[group], received[group]])
        out, index = (keep, group) if group < count // 2 else (send, group - count // 2)
        for head in range(KVH):
            out[index, head] = heads[head].astype(BF16)
        out[index, KVH] = encode(level)


def finish_kernel(tokens, *refs):
    parts, out = refs[:-1], refs[-1]
    heads, _ = merge([part[0] for part in parts])
    for head in range(KVH):
        for inner in range(QPK):
            start = (head * QPK + inner) * HD
            out[:, start:start + HD] = heads[head][inner * tokens:(inner + 1) * tokens, :].astype(BF16)


def settle_kernel(table, incoming, out, sem):
    def place(block, carry):
        pltpu.make_async_copy(incoming.at[table[1, block]], out.at[block], sem).start()
        return carry

    lax.fori_loop(0, out.shape[0], place, 0)
    pltpu.make_async_copy(incoming.at[pl.ds(0, out.shape[0])], out, sem).wait()


def on_device(
    saved_hidden, kv_weight, queries, new_kv, hist_blocks, new_len, pack_order, holder_slot
):
    count = lax.axis_size("req")
    hold, block_rows, width = saved_hidden.shape
    pair_width = kv_weight.shape[1]
    owned = holder_slot.shape[0] // count
    capacity = hold // count
    tokens, query_width = queries.shape
    groups = count // LAYER
    span = QPK * tokens
    wave = jnp.asarray(frequencies())

    def swap(value, flip):
        return lax.ppermute(value, "req", [(i, i ^ flip) for i in range(count)])

    layers = [queries] + [swap(queries, LAYER * group) for group in range(1, groups)]
    chunks = len(split_sizes(width))
    pairs, table, tags, turns = call(
        functools.partial(project_kernel, owned, capacity),
        "project",
        tuple(
            pltpu.with_memory_space_constraint(value, HBM)
            for value in (
                hist_blocks, pack_order, new_len, holder_slot.reshape(1, -1), wave, new_kv, saved_hidden, kv_weight
            )
        ),
        (HBM,) * 8,
        (
            ((hold + 1, block_rows, pair_width), BF16),
            ((8, HD), I32),
            ((16 + groups, hold * block_rows), F32),
            ((groups, 2, 8, HD), F32),
        ),
        (VM,) * 4,
        (
            VM((hold, block_rows, width), BF16),
            VM((width, pair_width), BF16),
            VM((hold * block_rows, pair_width), F32),
            VM((block_rows, pair_width), F32),
            SM(hist_blocks.shape, I32),
            SM(pack_order.shape, I32),
            SM(new_len.shape, I32),
            VM((1, holder_slot.shape[0]), I32),
            VM(wave.shape, F32),
            VM(new_kv.shape, BF16),
            pltpu.SemaphoreType.DMA((6,)),
            pltpu.SemaphoreType.DMA((chunks,)),
            pltpu.SemaphoreType.DMA((chunks,)),
        ),
        34,
    )
    outgoing, turned = call(
        functools.partial(ship_kernel, groups),
        "ship",
        (table, pairs, turns, *layers),
        (ANY,) + (VM,) * (groups + 2),
        (
            ((hold, block_rows, pair_width), BF16),
            ((KVH, groups, span, HD), BF16),
        ),
        (ANY, VM),
        (
            VM((groups, KVH * span, HD), F32),
            SM((8, HD), I32),
            pltpu.SemaphoreType.DMA(()),
            pltpu.SemaphoreType.DMA(()),
        ),
    )
    outgoing, pairs, turned = lax.optimization_barrier((outgoing, pairs, turned))
    pairs_beside = swap(pairs, 1)
    turned_across = swap(turned, 2)
    backwards = [list(range(count))[::-1]]
    incoming = lax.all_to_all(
        outgoing, "req", split_axis=0, concat_axis=0, axis_index_groups=backwards, tiled=True
    )
    share = ((groups, KVH + 1, span, HD), BF16)
    keep, send = call(
        functools.partial(attend_kernel, groups, tokens),
        "attend",
        (turned, turned_across, pairs, pairs_beside, tags),
        (VM,) * 5,
        (share, share),
        (VM, VM),
        mib=24,
        work=ATTEND_WORK,
    )
    step, left = 2, groups
    while left > 1:
        left //= 2
        share = ((left, KVH + 1, span, HD), BF16)
        keep, send = call(fold_kernel, "fold", (keep, swap(send, step)), (VM, VM), (share, share), (VM, VM))
        step *= 2
    parts = [keep, swap(send, step)]
    (restored,) = call(
        settle_kernel,
        "settle",
        (table, incoming),
        (SM, ANY),
        (((owned, block_rows, pair_width), BF16),),
        (ANY,),
        (pltpu.SemaphoreType.DMA(()),),
    )
    parts, restored = lax.optimization_barrier((parts, restored))
    (attention,) = call(
        functools.partial(finish_kernel, tokens),
        "finish",
        tuple(parts),
        (VM, VM),
        (((tokens, query_width), BF16),),
        (VM,),
    )
    return restored, attention


def solution(mesh):
    return jax.shard_map(
        on_device,
        mesh=mesh,
        in_specs=(
            P(("groups", "req"), None, None),
            P(),
            P(("groups", "req"), None),
            P(("groups", "req"), None),
            P("groups"),
            P("groups"),
            P("groups"),
            P("groups"),
        ),
        out_specs=(P(("groups", "req"), None, None), P(("groups", "req"), None)),
        check_vma=False,
    )
```

```python
import functools

import jax
import jax.numpy as jnp
import numpy as np
from jax import lax
from jax.experimental import pallas as pl
from jax.experimental.pallas import tpu as pltpu
from jax.sharding import PartitionSpec as P

KVH = 4
QPK = 8
HD = 128
NEWT = 16
ROPE_BASE = 500000.0
MASKED = -1e30
SCALE = HD ** -0.5
F32 = jnp.float32
BF16 = jnp.bfloat16
I32 = jnp.int32
HALF = KVH * HD
LAYER = 4
ATTEND_WORK = 60 * 10**9
VM = pltpu.VMEM
SM = pltpu.SMEM
ANY = pl.ANY
HBM = pltpu.HBM


def frequencies():
    wave = ROPE_BASE ** (-(np.arange(HD // 2, dtype=np.float64) * 2.0 / HD))
    return np.concatenate([wave, wave]).astype(np.float32)[None, :]


def lane_sign(shape):
    lanes = lax.broadcasted_iota(I32, shape, len(shape) - 1)
    return jnp.where(lanes < HD // 2, -1.0, 1.0).astype(F32)


def specs(*spaces):
    return [pl.BlockSpec(memory_space=space) for space in spaces]


def call(kernel, name, inputs, spaces, outputs, out_spaces, scratch=(), mib=16, work=0):
    return pl.pallas_call(
        kernel,
        out_shape=tuple(jax.ShapeDtypeStruct(shape, kind) for shape, kind in outputs),
        in_specs=specs(*spaces),
        out_specs=tuple(specs(*out_spaces)),
        scratch_shapes=list(scratch),
        compiler_params=pltpu.CompilerParams(vmem_limit_bytes=mib << 20),
        cost_estimate=pl.CostEstimate(flops=work, transcendentals=0, bytes_accessed=0) if work else None,
        name=name,
    )(*inputs)


def split_sizes(width):
    return tuple(width // 16 * units for units in (1, 1, 2, 3, 3, 3, 2, 1))


def iota(shape, axis):
    return lax.broadcasted_iota(I32, shape, axis)


def lane_total(values):
    return jnp.sum(values, axis=1, keepdims=True)


def spans(hist_ref, pack_ref):
    start = jnp.int32(0)
    for position in range(hist_ref.shape[0]):
        which = pack_ref[position]
        stop = start + hist_ref[which]
        yield which, start, stop
        start = stop


def seat(device, count):
    back = count - 1 - device
    return back ^ ((back < count // 2) * (count // 4))


def places(device, holder, hist_ref, pack_ref, hold, owned, capacity):
    total = holder.shape[1]
    count = hold // capacity
    local = holder - device * hold
    held = (local >= 0) & (local < hold)
    blocks = iota((hold, total), 1)
    here = local == iota((hold, total), 0)
    block = lane_total(jnp.where(here, blocks, 0).astype(F32)).astype(I32)
    owner = block // owned
    rank = lane_total(jnp.where(held & (blocks < block) & (blocks >= owner * owned), 1.0, 0.0)).astype(I32)
    target = jnp.minimum(seat(owner, count) * capacity + jnp.minimum(rank, capacity - 1), hold - 1)
    target = jnp.where(lane_total(jnp.where(here, 1.0, 0.0)) > 0, target, iota((hold, 1), 0))
    depth = jnp.zeros((hold, 1), I32)
    for _, start, stop in spans(hist_ref, pack_ref):
        depth = jnp.where((block >= start) & (block < stop), block - start, depth)
    mine = device * owned
    blocks = iota((owned, total), 1)
    rows = iota((owned, total), 0) + mine
    keeper = holder // hold
    kept = lane_total(jnp.where(blocks == rows, keeper, 0).astype(F32)).astype(I32)
    order = lane_total(jnp.where((keeper == kept) & (blocks >= mine) & (blocks < rows), 1.0, 0.0)).astype(I32)
    arrival = seat(kept, count) * capacity + jnp.minimum(order, capacity - 1)
    arrival = jnp.concatenate([arrival, jnp.zeros((hold - owned, 1), I32)], axis=0)
    diagonal = iota((hold, HD), 0) == iota((hold, HD), 1)
    rows = [jnp.sum(jnp.where(diagonal, column, 0).astype(F32), axis=0, keepdims=True) for column in (target, arrival)]
    table = jnp.concatenate(rows + [jnp.zeros((6, HD), F32)], axis=0).astype(I32)
    return table, depth


def row_tags(device, holder, hist_ref, pack_ref, hold, block_rows):
    total = holder.shape[1]
    blocks = iota((8, total), 1)
    request = jnp.zeros((8, total), F32)
    for which, start, stop in spans(hist_ref, pack_ref):
        request = jnp.where((blocks >= start) & (blocks < stop), (which + 1).astype(F32), request)
    local = holder - device * hold
    match = local == iota((hold * block_rows, total), 0) // block_rows
    return lax.dot_general(
        request.astype(BF16), match.astype(F32).astype(BF16), (((1,), (1,)), ((), ())), preferred_element_type=F32
    )


def project_kernel(owned, capacity, hist_hbm, pack_hbm, len_hbm, holder_hbm, wave_hbm, new_hbm, rows_hbm, weight_hbm,
                   pairs, table_out, tags, turns,
                   rows_buf, weight_buf, total, fresh, hist_ref, pack_ref, len_ref, holder_ref, wave_ref, new_ref,
                   small_sem, rows_sem, weight_sem):
    hold, block_rows, width = rows_hbm.shape
    small = [
        pltpu.make_async_copy(source, target, small_sem.at[index])
        for index, (source, target) in enumerate((
            (hist_hbm, hist_ref), (pack_hbm, pack_ref), (len_hbm, len_ref), (holder_hbm, holder_ref),
            (wave_hbm, wave_ref), (new_hbm, new_ref),
        ))
    ]
    for copy in small:
        copy.start()
    copies, offset = [], 0
    for part, size in enumerate(split_sizes(width)):
        span = pl.ds(offset, size)
        copies.append((
            offset,
            size,
            pltpu.make_async_copy(weight_hbm.at[span, :], weight_buf.at[span, :], weight_sem.at[part]),
            pltpu.make_async_copy(rows_hbm.at[:, :, span], rows_buf.at[:, :, span], rows_sem.at[part]),
        ))
        offset += size

    def depart(part):
        if part < len(copies):
            for copy in copies[part][2:]:
                copy.start()

    depart(0)
    depart(1)
    depart(2)

    def multiply(part, lanes):
        offset, size, _, _ = copies[part]
        left = rows_buf[:, :, offset:offset + size].reshape(hold * block_rows, size)
        product = jnp.dot(left, weight_buf[offset:offset + size, lanes], preferred_element_type=F32)
        return product if part == 0 else total[:, lanes] + product

    def arrive(part):
        for copy in copies[part][2:]:
            copy.wait()
        depart(part + 3)

    everything = slice(0, 2 * HALF)
    for part in range(2):
        arrive(part)
        total[...] = multiply(part, everything)
    for copy in small:
        copy.wait()
    device = lax.axis_index("req")
    holder = holder_ref[...]
    found, depth = places(device, holder, hist_ref, pack_ref, hold, owned, capacity)
    table_out[...] = found
    tags[0:8, :] = row_tags(device, holder, hist_ref, pack_ref, hold, block_rows)
    tags[8:16, :] = row_tags(device ^ 1, holder, hist_ref, pack_ref, hold, block_rows)
    wave = wave_ref[...]
    sign = lane_sign((block_rows, HD))
    angle = (depth * block_rows).astype(F32) * wave
    block_cos, block_sin = jnp.cos(angle)[:, None, :], jnp.sin(angle)[:, None, :]
    angle = iota((block_rows, HD), 0).astype(F32) * wave
    row_cos, row_sin = jnp.cos(angle)[None], jnp.sin(angle)[None]
    cosine = (block_cos * row_cos - block_sin * row_sin).reshape(-1, HD)
    sine = ((block_sin * row_cos + block_cos * row_sin) * sign[None]).reshape(-1, HD)
    tokens = new_ref.shape[0]
    first = device * tokens
    place = iota((block_rows, HD), 0) + (hist_ref[first // NEWT] * block_rows + first % NEWT)
    angle = place.astype(F32) * wave
    new_cos, new_sin = jnp.cos(angle), jnp.sin(angle) * sign
    for group in range(turns.shape[0]):
        request = (first // NEWT) ^ group
        place = iota((8, HD), 0) % tokens + (hist_ref[request] * block_rows + first % NEWT)
        angle = place.astype(F32) * wave
        turns[group, 0] = jnp.cos(angle)
        turns[group, 1] = jnp.sin(angle) * lane_sign((8, HD))
        tags[pl.ds(16 + group, 1), :] = jnp.full((1, tags.shape[1]), len_ref[request].astype(F32))
    fresh[...] = jnp.zeros_like(fresh)
    fresh[0:tokens, :] = new_ref[...].astype(F32)
    for head in range(KVH):
        lanes = slice(head * HD, (head + 1) * HD)
        part = fresh[:, lanes]
        pairs[hold, :, lanes] = (part * new_cos + pltpu.roll(part, HD // 2, 1) * new_sin).astype(BF16)
    pairs[hold, :, HALF:] = fresh[:, HALF:].astype(BF16)
    last = len(copies) - 1
    for part in range(2, last):
        arrive(part)
        total[...] = multiply(part, everything)
    arrive(last)
    for head in range(2 * KVH):
        lanes = slice(head * HD, (head + 1) * HD)
        if head % KVH == 0:
            half = slice(head * HD, (head + KVH) * HD)
            total[:, half] = multiply(last, half)
        part = total[:, lanes]
        if head < KVH:
            part = part * cosine + pltpu.roll(part, HD // 2, 1) * sine
        pairs[0:hold, :, lanes] = part.astype(BF16).reshape(hold, block_rows, HD)


def ship_kernel(groups, table_hbm, pairs, turns, *refs):
    queries, (outgoing, turned, rows, table, table_sem, send_sem) = refs[:groups], refs[groups:]
    table_copy = pltpu.make_async_copy(table_hbm, table, table_sem)
    table_copy.start()
    hold = outgoing.shape[0]
    tokens = queries[0].shape[0]

    def turn(group):
        values = queries[group][...].astype(F32)
        for head in range(KVH * QPK):
            rows[group, pl.ds(head * tokens, tokens), :] = values[:, head * HD:(head + 1) * HD]
        flat = rows[group]
        swapped = pltpu.roll(flat, HD // 2, 1)
        result = flat.reshape(-1, 8, HD) * turns[group, 0][None] + swapped.reshape(-1, 8, HD) * turns[group, 1][None]
        turned[:, group] = result.reshape(KVH, QPK * tokens, HD).astype(BF16)

    for group in range(groups // 2):
        turn(group)
    table_copy.wait()

    def send(slot, carry):
        pltpu.make_async_copy(pairs.at[slot], outgoing.at[table[0, slot]], send_sem).start()
        return carry

    lax.fori_loop(0, hold, send, 0)
    for group in range(groups // 2, groups):
        turn(group)
    pltpu.make_async_copy(pairs.at[pl.ds(0, hold)], outgoing, send_sem).wait()


def encode(level):
    lanes = iota(level.shape, 1)
    high = level.astype(BF16).astype(F32)
    rest = level - high
    middle = rest.astype(BF16).astype(F32)
    low = rest - middle
    packed = jnp.where(lanes < 32, high, jnp.where(lanes < 64, pltpu.roll(middle, 32, 1), pltpu.roll(low, 64, 1)))
    return jnp.where(lanes < 96, packed, 0.0).astype(BF16)


def decode(packed):
    packed = packed.astype(F32)
    return packed + (pltpu.roll(packed, HD - 32, 1) + pltpu.roll(packed, HD - 64, 1))


def folding_order(groups):
    if groups == 1:
        return [0]
    inner = folding_order(groups // 2)
    return [2 * group for group in inner] + [2 * group + 1 for group in inner]


def attend_kernel(groups, tokens, queries, queries_across, pairs, pairs_beside, tags, keep, send):
    hold, block_rows = pairs.shape[0] - 1, pairs.shape[1]
    rows_kept = hold * block_rows
    span = QPK * tokens
    rows = 2 * groups * span
    device = lax.axis_index("req")
    per_request = NEWT // tokens
    request = device // per_request
    row = iota((rows, 1), 0)
    group = (row // span) % groups
    wanted = ((request ^ group) + 1).astype(F32)
    tag_rows = [tags[0:1, :], tags[8:9, :]]
    row_all = iota((rows, 2 * block_rows), 0)
    column = iota((rows, 2 * block_rows), 1)
    across = row_all // (groups * span)
    query_place = ((device ^ (2 * across)) % per_request) * tokens + row_all % tokens
    key_index = column % block_rows
    key_place = ((device ^ (column // block_rows)) % per_request) * tokens + key_index
    fresh_ok = (
        ((row_all // span) % groups == 0) & (key_index < tokens) & (key_place <= query_place)
        & (key_place.astype(F32) < tags[16:17, 0:1])
    )
    limit = jnp.zeros((rows, 1), F32)
    for layer in range(groups):
        limit = jnp.where(group == layer, tags[16 + layer:17 + layer, 0:1], limit)
    side = row // (groups * span)
    live = (((device ^ (2 * side)) % per_request) * tokens + row % tokens).astype(F32) < limit
    lanes = iota((rows, HD), 1)
    levels = jnp.zeros((rows, HD), F32)
    for head in range(KVH):
        key_lanes = slice(head * HD, (head + 1) * HD)
        value_lanes = slice(HALF + head * HD, HALF + (head + 1) * HD)
        query = jnp.concatenate(
            [queries[head].reshape(groups * span, HD), queries_across[head].reshape(groups * span, HD)], axis=0
        )
        scores, values = [], []
        for source, tag in zip((pairs, pairs_beside), tag_rows):
            keys = source[0:hold, :, key_lanes].reshape(rows_kept, HD)
            part = lax.dot_general(query, keys, (((1,), (1,)), ((), ())), preferred_element_type=F32) * SCALE
            scores.append(jnp.where(tag == wanted, part, MASKED))
            values.append(source[0:hold, :, value_lanes].reshape(rows_kept, HD))
        keys = jnp.concatenate([pairs[hold, :, key_lanes], pairs_beside[hold, :, key_lanes]], axis=0)
        part = lax.dot_general(query, keys, (((1,), (1,)), ((), ())), preferred_element_type=F32) * SCALE
        scores.append(jnp.where(fresh_ok, part, MASKED))
        values.append(jnp.concatenate([pairs[hold, :, value_lanes], pairs_beside[hold, :, value_lanes]], axis=0))
        peak = jnp.max(jnp.maximum(scores[0], scores[1]), axis=1, keepdims=True)
        peak = jnp.maximum(peak, jnp.max(scores[2], axis=1, keepdims=True))
        weights = [jnp.exp(part - peak) for part in scores]
        denominator = lane_total(weights[0] + weights[1]) + lane_total(weights[2])
        sums = None
        for weight, value in zip(weights, values):
            part = jnp.dot(weight.astype(BF16), value, preferred_element_type=F32)
            sums = part if sums is None else sums + part
        sums = jnp.where(live, sums / denominator, 0.0).astype(BF16).reshape(2, groups, span, HD)
        for place, group in enumerate(folding_order(groups)):
            keep[place, head] = sums[0, group]
            send[place, head] = sums[1, group]
        levels = jnp.where(lanes == head, peak + jnp.log(denominator), levels)
    packed = encode(levels).reshape(2, groups, span, HD)
    for place, group in enumerate(folding_order(groups)):
        keep[place, KVH] = packed[0, group]
        send[place, KVH] = packed[1, group]


def merge(parts):
    levels = [decode(part[KVH]) for part in parts]
    top = functools.reduce(jnp.maximum, levels)
    scales = [jnp.exp(level - top) for level in levels]
    whole = functools.reduce(jnp.add, scales)
    scales = [scale / whole for scale in scales]
    heads = []
    for head in range(KVH):
        pieces = [part[head].astype(F32) * scale[:, head:head + 1] for part, scale in zip(parts, scales)]
        heads.append(functools.reduce(jnp.add, pieces))
    return heads, top + jnp.log(whole)


def fold_kernel(kept, received, keep, send):
    count = kept.shape[0]
    for group in range(count):
        heads, level = merge([kept[group], received[group]])
        out, index = (keep, group) if group < count // 2 else (send, group - count // 2)
        for head in range(KVH):
            out[index, head] = heads[head].astype(BF16)
        out[index, KVH] = encode(level)


def finish_kernel(tokens, *refs):
    parts, out = refs[:-1], refs[-1]
    heads, _ = merge([part[0] for part in parts])
    for head in range(KVH):
        for inner in range(QPK):
            start = (head * QPK + inner) * HD
            out[:, start:start + HD] = heads[head][inner * tokens:(inner + 1) * tokens, :].astype(BF16)


def settle_kernel(table, incoming, out, sem):
    def place(block, carry):
        pltpu.make_async_copy(incoming.at[table[1, block]], out.at[block], sem).start()
        return carry

    lax.fori_loop(0, out.shape[0], place, 0)
    pltpu.make_async_copy(incoming.at[pl.ds(0, out.shape[0])], out, sem).wait()


def on_device(
    saved_hidden, kv_weight, queries, new_kv, hist_blocks, new_len, pack_order, holder_slot
):
    count = lax.axis_size("req")
    hold, block_rows, width = saved_hidden.shape
    pair_width = kv_weight.shape[1]
    owned = holder_slot.shape[0] // count
    capacity = hold // count
    tokens, query_width = queries.shape
    groups = count // LAYER
    span = QPK * tokens
    wave = jnp.asarray(frequencies())

    def swap(value, flip):
        return lax.ppermute(value, "req", [(i, i ^ flip) for i in range(count)])

    layers = [queries] + [swap(queries, LAYER * group) for group in range(1, groups)]
    chunks = len(split_sizes(width))
    pairs, table, tags, turns = call(
        functools.partial(project_kernel, owned, capacity),
        "project",
        tuple(
            pltpu.with_memory_space_constraint(value, HBM)
            for value in (
                hist_blocks, pack_order, new_len, holder_slot.reshape(1, -1), wave, new_kv, saved_hidden, kv_weight
            )
        ),
        (HBM,) * 8,
        (
            ((hold + 1, block_rows, pair_width), BF16),
            ((8, HD), I32),
            ((16 + groups, hold * block_rows), F32),
            ((groups, 2, 8, HD), F32),
        ),
        (VM,) * 4,
        (
            VM((hold, block_rows, width), BF16),
            VM((width, pair_width), BF16),
            VM((hold * block_rows, pair_width), F32),
            VM((block_rows, pair_width), F32),
            SM(hist_blocks.shape, I32),
            SM(pack_order.shape, I32),
            SM(new_len.shape, I32),
            VM((1, holder_slot.shape[0]), I32),
            VM(wave.shape, F32),
            VM(new_kv.shape, BF16),
            pltpu.SemaphoreType.DMA((6,)),
            pltpu.SemaphoreType.DMA((chunks,)),
            pltpu.SemaphoreType.DMA((chunks,)),
        ),
        34,
    )
    outgoing, turned = call(
        functools.partial(ship_kernel, groups),
        "ship",
        (table, pairs, turns, *layers),
        (ANY,) + (VM,) * (groups + 2),
        (
            ((hold, block_rows, pair_width), BF16),
            ((KVH, groups, span, HD), BF16),
        ),
        (ANY, VM),
        (
            VM((groups, KVH * span, HD), F32),
            SM((8, HD), I32),
            pltpu.SemaphoreType.DMA(()),
            pltpu.SemaphoreType.DMA(()),
        ),
    )
    outgoing, pairs, turned = lax.optimization_barrier((outgoing, pairs, turned))
    pairs_beside = swap(pairs, 1)
    turned_across = swap(turned, 2)
    seats = [sorted(range(count), key=lambda member: seat(member, count))]
    incoming = lax.all_to_all(
        outgoing, "req", split_axis=0, concat_axis=0, axis_index_groups=seats, tiled=True
    )
    share = ((groups, KVH + 1, span, HD), BF16)
    keep, send = call(
        functools.partial(attend_kernel, groups, tokens),
        "attend",
        (turned, turned_across, pairs, pairs_beside, tags),
        (VM,) * 5,
        (share, share),
        (VM, VM),
        mib=24,
        work=ATTEND_WORK,
    )
    step, left = 2, groups
    while left > 1:
        left //= 2
        share = ((left, KVH + 1, span, HD), BF16)
        keep, send = call(fold_kernel, "fold", (keep, swap(send, step)), (VM, VM), (share, share), (VM, VM))
        step *= 2
    parts = [keep, swap(send, step)]
    (restored,) = call(
        settle_kernel,
        "settle",
        (table, incoming),
        (SM, ANY),
        (((owned, block_rows, pair_width), BF16),),
        (ANY,),
        (pltpu.SemaphoreType.DMA(()),),
    )
    parts, restored = lax.optimization_barrier((parts, restored))
    (attention,) = call(
        functools.partial(finish_kernel, tokens),
        "finish",
        tuple(parts),
        (VM, VM),
        (((tokens, query_width), BF16),),
        (VM,),
    )
    return restored, attention


def solution(mesh):
    return jax.shard_map(
        on_device,
        mesh=mesh,
        in_specs=(
            P(("groups", "req"), None, None),
            P(),
            P(("groups", "req"), None),
            P(("groups", "req"), None),
            P("groups"),
            P("groups"),
            P("groups"),
            P("groups"),
        ),
        out_specs=(P(("groups", "req"), None, None), P(("groups", "req"), None)),
        check_vma=False,
    )
```
